256 devices in a mesh: dp: 64 (over x, y, z_lo, core), fsdp: 4 (over z_hi).
Axes of the slice: x: 4, y: 4, z: 8 (z_hi: 4, z_lo: 2; z = z_hi * 2 + z_lo), core: 2. Of those that a mesh axis runs over, the one named last changes fastest.
Arguments:
- momentum: float32 [64, 64, 28672], P('dp', None, 'fsdp'), may hold values from -6 to 6
- gradient: bfloat16 [64, 64, 28672], P('dp', None, 'fsdp'), may hold values from -6 to 6
- weight: bfloat16 [64, 28672], P(None, 'fsdp'), may hold values from -0.75 to 0.75
- tokens: bfloat16 [32768, 64], P(('dp', 'fsdp')), may hold values from -6 to 6
- block_index: int32 [64, 1, 448, 4], P('dp', None, 'fsdp'), may hold values from 0 to 63, all different within a row
Outputs:
- new_momentum: float32 [64, 64, 28672], P('dp', None, 'fsdp')
- preact: bfloat16 [32768, 28672], P(('dp', 'fsdp'))
The draws below stay inside these ranges and needn't reach their ends.
Inputs may be any that keep to these rules, and one draw needn't show every extreme that they name: Within each group the 4 entries of block_index name different blocks.
All inputs are finite; a program needn't handle non-finite values.
Results may differ from the reference program's by a relative error of at most 0.0049.
Values may be sent and summed in bfloat16 or wider, within the bound.
No kernel may reach another device: no remote copies, remote signals or barrier semaphores. Data moves between devices by JAX's collectives and lax.ppermute only.
A program may use at most 192 MiB of HBM per device.

```python
import jax
import jax.numpy as jnp
from jax import lax

FF = 28672
SLAB_ROWS = 64
GROUP = 64
BLOCK = 8
KEEP = 4
POSITIONS = 64
GROUP_ROWS = 1
GROUP_COLS = 448
TOKENS = 32768
N_DP = 64


def block_scale(stream_key, extent, cuts, smallest, top_value):
    loudness, own = 1.0, jax.random.fold_in(stream_key, 6)
    for dim, blocks in cuts:
        steps = jnp.exp(jax.random.uniform(jax.random.fold_in(own, dim), (blocks,), jnp.float32, smallest / len(cuts), top_value / len(cuts)))
        loudness = loudness * jnp.repeat(steps, extent[dim] // blocks).reshape([-1 if axis == dim else 1 for axis in range(len(extent))])
    return loudness


def choose_distinct(key, rows, number_of, top, lift):
    ranking = jax.random.permutation(jax.random.fold_in(key, 1), number_of)
    favour = ranking
    for power in range(3):
        favour = favour * favour // number_of
    favour = favour * lift // number_of
    lots = jax.random.randint(jax.random.fold_in(key, 2), (rows, number_of), 0, 4096) + favour
    fixed_rows = jax.random.permutation(jax.random.fold_in(key, 3), rows)[jnp.arange(number_of) % rows]
    lots = jnp.where(jnp.arange(rows)[:, None] == fixed_rows[None, :], 1 << 14, lots)
    priority = lots * number_of + jnp.arange(number_of)
    return lax.top_k(priority.astype(jnp.int32), top)[1].astype(jnp.int32)


def bell_draw(rng, shape, deviation, most, split=(), kind=jnp.bfloat16):
    array = deviation * jax.random.normal(rng, shape, jnp.float32)
    if split:
        array = array * block_scale(rng, shape, split, -0.22, 0.18)
    return jnp.clip(array, -most, most).astype(kind)


def setup_inputs(seed: int = 0) -> dict:
    key_list = jax.random.split(jax.random.key(seed), 6)
    return {
        "momentum": bell_draw(key_list[0], (N_DP, SLAB_ROWS, FF), 1.0, 6.0, ((0, 64), (2, 4)), jnp.float32),
        "gradient": bell_draw(key_list[1], (N_DP, SLAB_ROWS, FF), 1.0, 6.0, ((0, 64), (2, 4))),
        "weight": bell_draw(key_list[2], (SLAB_ROWS, FF), SLAB_ROWS ** -0.5, 0.75, ((1, 4),)),
        "tokens": bell_draw(key_list[3], (TOKENS, SLAB_ROWS), 1.0, 6.0, ((0, 256),)),
        "block_index": choose_distinct(key_list[4], N_DP * GROUP_ROWS * GROUP_COLS, POSITIONS, KEEP, 0).reshape((N_DP, GROUP_ROWS, GROUP_COLS, KEEP)),
    }


decay_rate = 0.9
step_scale = 5.0
exact = lax.Precision.HIGHEST

def cosine_table(group_size):
    position = jnp.arange(group_size, dtype=jnp.float32)
    frequency = position[:, None]
    factor = jnp.where(frequency == 0, jnp.sqrt(1.0 / group_size), jnp.sqrt(2.0 / group_size))
    return factor * jnp.cos(jnp.pi * (2.0 * position[None, :] + 1.0) * frequency / (2.0 * group_size))

def group_transform(field_grid, left_table, right_table, group_size):
    height, breadth = field_grid.shape
    stacked = field_grid.reshape(height // group_size, group_size, breadth)
    mixed = jnp.einsum('ka,rac->rkc', left_table, stacked, precision=exact)
    span = right_table.shape[0]
    result = jnp.dot(mixed.reshape(-1, span), right_table, precision=exact)
    return result.reshape(height, breadth)

def to_blocks(field_grid, group_size, block_size):
    height, breadth = field_grid.shape
    per_side = group_size // block_size
    shaped = field_grid.reshape(height // group_size, per_side, block_size, breadth // group_size, per_side, block_size)
    shaped = shaped.transpose(0, 3, 1, 4, 2, 5)
    return shaped.reshape(height // group_size * (breadth // group_size), per_side * per_side, block_size * block_size)

def from_blocks(blocks, height, breadth, group_size, block_size):
    per_side = group_size // block_size
    shaped = blocks.reshape(height // group_size, breadth // group_size, per_side, per_side, block_size, block_size)
    shaped = shaped.transpose(0, 2, 4, 1, 3, 5)
    return shaped.reshape(height, breadth)

def reference(momentum, gradient, weight, tokens, block_index):
    cosines = cosine_table(GROUP)

    def replica_step(summed, inputs):
        moment_old, grad_rows, picked = inputs
        moment = decay_rate * moment_old + grad_rows.astype(jnp.float32)
        coefficients = to_blocks(group_transform(moment, cosines, cosines.T, GROUP), GROUP, BLOCK)
        chosen = jax.nn.one_hot(picked.reshape(-1, KEEP), POSITIONS, dtype=jnp.float32)
        block_mask = lax.optimization_barrier(jnp.sum(chosen, axis=1))
        retained = coefficients * block_mask[:, :, None]
        transmitted = group_transform(from_blocks(retained, SLAB_ROWS, FF, GROUP, BLOCK), cosines.T, cosines, GROUP)
        return (summed + retained, moment - transmitted)
    start_grid = jnp.zeros((GROUP_ROWS * GROUP_COLS, POSITIONS, BLOCK * BLOCK), jnp.float32)
    summed, new_momentum = lax.scan(replica_step, start_grid, (momentum, gradient, block_index))
    update = group_transform(from_blocks(summed / N_DP, SLAB_ROWS, FF, GROUP, BLOCK), cosines.T, cosines, GROUP)
    new_weight = (weight.astype(jnp.float32) - step_scale * update).astype(jnp.bfloat16)
    preact = jnp.dot(tokens, new_weight, preferred_element_type=jnp.float32).astype(jnp.bfloat16)
    return (new_momentum, preact)
```

```python
import jax
import jax.numpy as jnp
import ml_dtypes
import numpy as np
from jax import lax
from jax.experimental import pallas as pl
from jax.experimental.pallas import tpu as pltpu
from jax.sharding import Mesh
from jax.sharding import PartitionSpec as P

GROUP = 64
BLOCK = 8
KEEP = 4
LANES = 128
ROWS = 16
DECAY = 0.9
STEP = 5.0
VMEM = 60 * 2**20
F32 = jnp.float32
BF16 = jnp.bfloat16
AXES = ("x", "y", "zl", "core", "fsdp")
SIZES = (4, 4, 2, 2)


def halves(table):
    high = table.astype(ml_dtypes.bfloat16)
    low = (table - high.astype(np.float64)).astype(ml_dtypes.bfloat16)
    return high, low


def cosine_table():
    position = np.arange(GROUP, dtype=np.float64)
    frequency = position[:, None]
    factor = np.where(frequency == 0, np.sqrt(1.0 / GROUP), np.sqrt(2.0 / GROUP))
    return factor * np.cos(np.pi * (2.0 * position[None, :] + 1.0) * frequency / (2.0 * GROUP))


def left_operand(table):
    high, low = halves(table)
    return np.concatenate([high, high, low, low], axis=1)


def right_operand(table):
    high, low = halves(np.kron(np.eye(LANES // GROUP), table))
    return np.block([[high, low], [high, low]])


def split(value):
    high = value.astype(BF16)
    return high, (value - high.astype(F32)).astype(BF16)


def mix_rows(operand, value):
    high, low = split(value)
    return jnp.dot(
        operand, jnp.concatenate([high, low, high, low], axis=0), preferred_element_type=F32
    )


def mix_columns(value, operand):
    high, low = split(value)
    both = jnp.dot(
        jnp.concatenate([high, low], axis=1), operand, preferred_element_type=F32
    )
    return both[:, :LANES] + both[:, LANES:]


def compress_kernel(
    first, tiles, place, picked, momentum, gradient, weight, row_fwd, col_fwd, row_inv, col_inv, *rest
):
    if first:
        new_momentum, sent, own_weight = rest
    else:
        _, new_momentum, sent = rest
    step = pl.program_id(0)
    core = place[2]
    half = (1 - core) if first else core
    moment = DECAY * momentum[0] + gradient[0].astype(F32)
    mixed = mix_rows(row_fwd[...], moment)
    stacked = jnp.concatenate(
        [mixed[:, t * LANES : (t + 1) * LANES] for t in range(tiles)], axis=0
    )
    coefficients = mix_columns(stacked, col_fwd[...])
    lane = lax.broadcasted_iota(jnp.int32, (BLOCK, LANES), 1)
    lane_block = (lane % GROUP) // BLOCK
    left_group = lane < GROUP
    row_block = lax.broadcasted_iota(jnp.int32, (GROUP // BLOCK, BLOCK, LANES), 0) * BLOCK
    start = (half * pl.num_programs(0) + step) * tiles * (LANES // GROUP)
    kept = []
    for t in range(tiles):
        mask = None
        for k in range(KEEP):
            wanted = jnp.where(
                left_group, picked[k, start + 2 * t], picked[k, start + 2 * t + 1]
            ) - lane_block
            hit = wanted[None] == row_block
            mask = hit if mask is None else mask | hit
        part = coefficients[t * GROUP : (t + 1) * GROUP].reshape(GROUP // BLOCK, BLOCK, LANES)
        kept.append(jnp.where(mask, part, 0.0).reshape(GROUP, LANES))
    unmixed = mix_columns(jnp.concatenate(kept, axis=0), col_inv[...])
    spread = jnp.concatenate(
        [unmixed[t * GROUP : (t + 1) * GROUP] for t in range(tiles)], axis=1
    )
    transmitted = mix_rows(row_inv[...], spread)
    new_momentum[0] = moment - transmitted
    for i in range(GROUP // ROWS):
        for t in range(tiles):
            sent[i, 0, t] = transmitted[i * ROWS : (i + 1) * ROWS, t * LANES : (t + 1) * LANES]
    if first:

        @pl.when(step == 0)
        def _():
            for t in range(tiles):
                own_weight[t] = weight[:, t * LANES : (t + 1) * LANES].astype(F32)


def compress(first, place, picked, momentum, gradient, weight, tables, partial=None):
    height, breadth = weight.shape
    steps = SIZES[1]
    wide = breadth // 2 // steps
    tiles = wide // LANES
    chunk = (tiles, ROWS, LANES)

    def columns(i, place, picked):
        half = (1 - place[2]) if first else place[2]
        return (0, 0, half * steps + i)

    fixed = lambda i, place, picked: (0, 0)
    slab = pl.BlockSpec((1, height, wide), columns)
    in_specs = [
        slab,
        slab,
        pl.BlockSpec((ROWS, wide), lambda i, place, picked: (place[0], place[2] * steps + place[1])),
    ] + [pl.BlockSpec(table.shape, fixed) for table in tables]
    out_shape = [
        jax.ShapeDtypeStruct((1, height, breadth), F32),
        jax.ShapeDtypeStruct((SIZES[0], steps) + chunk, F32),
    ]
    out_specs = [
        slab,
        pl.BlockSpec((SIZES[0], 1) + chunk, lambda i, place, picked: (0, i, 0, 0, 0)),
    ]
    operands = [place, picked, momentum, gradient, weight, *tables]
    aliases = {}
    if first:
        out_shape.append(jax.ShapeDtypeStruct(chunk, F32))
        out_specs.append(pl.BlockSpec(chunk, lambda i, place, picked: (0, 0, 0)))
    else:
        aliases = {len(operands): 0}
        operands.append(partial)
        in_specs.append(pl.BlockSpec(memory_space=pl.ANY))

    def body(*refs):
        compress_kernel(first, tiles, *refs)

    return pl.pallas_call(
        body,
        grid_spec=pltpu.PrefetchScalarGridSpec(
            num_scalar_prefetch=2, grid=(steps,), in_specs=in_specs, out_specs=out_specs
        ),
        out_shape=out_shape,
        input_output_aliases=aliases,
        compiler_params=pltpu.CompilerParams(vmem_limit_bytes=VMEM),
        cost_estimate=pl.CostEstimate(
            flops=2 * 4 * 256 * height * breadth, bytes_accessed=6 * height * breadth, transcendentals=0
        ),
        name="compress_first" if first else "compress_second",
    )(*operands)


def project(first, place, tokens, pieces, breadth, partial=None):
    count, depth = tokens.shape
    _, side, shifts, tiles, rows, lanes = pieces.shape
    wide = tiles * lanes

    def out_columns(k, place):
        half = place[2] if first else 1 - place[2]
        return (0, lax.rem(place[3] - k + shifts, shifts) * 2 + half)

    def body(place, tokens, pieces, *rest):
        out = rest[-1]
        for j in range(side):
            table = jnp.concatenate(
                [pieces[:, j, 0, t].reshape(depth, lanes) for t in range(tiles)], axis=1
            )
            out[:, j * wide : (j + 1) * wide] = jnp.dot(
                tokens[...], table, preferred_element_type=F32
            ).astype(BF16)

    in_specs = [
        pl.BlockSpec((count, depth), lambda k, place: (0, 0)),
        pl.BlockSpec((SIZES[0], side, 1, tiles, rows, lanes), lambda k, place: (0, 0, k, 0, 0, 0)),
    ]
    operands = [place, tokens, pieces]
    aliases = {}
    if not first:
        aliases = {3: 0}
        operands.append(partial)
        in_specs.append(pl.BlockSpec(memory_space=pl.ANY))
    return pl.pallas_call(
        body,
        grid_spec=pltpu.PrefetchScalarGridSpec(
            num_scalar_prefetch=1,
            grid=(shifts,),
            in_specs=in_specs,
            out_specs=pl.BlockSpec((count, side * wide), out_columns),
        ),
        out_shape=jax.ShapeDtypeStruct((count, breadth), BF16),
        input_output_aliases=aliases,
        compiler_params=pltpu.CompilerParams(vmem_limit_bytes=VMEM),
        cost_estimate=pl.CostEstimate(
            flops=count * depth * breadth, bytes_accessed=count * breadth, transcendentals=0
        ),
        name="project_first" if first else "project_second",
    )(*operands)


def shift(value, axis, size, by):
    return lax.ppermute(value, axis, [(i, (i + by) % size) for i in range(size)])


def on_device(momentum, gradient, weight, tokens, block_index):
    fsdp = lax.axis_size("fsdp")
    breadth = weight.shape[1]
    place = jnp.stack([lax.axis_index(a) for a in ("x", "y", "core", "fsdp")]).astype(jnp.int32)
    picked = block_index[0, 0].T
    cosines = cosine_table()
    tables = [
        jnp.asarray(left_operand(cosines)),
        jnp.asarray(right_operand(cosines.T)),
        jnp.asarray(left_operand(cosines.T)),
        jnp.asarray(right_operand(cosines)),
    ]
    partial, away, own_weight = compress(True, place, picked, momentum, gradient, weight, tables)
    arrived = shift(away, "core", 2, 1)
    new_momentum, kept = compress(
        False, place, picked, momentum, gradient, weight, tables, partial
    )
    pair = (kept + arrived).astype(BF16)
    plane = SIZES[0] * SIZES[1]
    pair = pair.reshape((plane,) + pair.shape[2:])
    parts = lax.all_to_all(pair, ("x", "y"), 0, 0, tiled=True)
    summed = jnp.sum(parts.astype(F32), axis=0)
    total = summed + shift(summed, "zl", 2, 1)
    replicas = float(np.prod(SIZES))
    chunk = (own_weight - (STEP / replicas) * total).astype(BF16)
    row = jnp.stack([chunk] + [shift(chunk, "fsdp", fsdp, k) for k in range(1, fsdp)])
    pieces = lax.all_to_all(
        jnp.broadcast_to(row[None], (plane,) + row.shape), ("x", "y"), 0, 0, tiled=True
    ).reshape(SIZES[:2] + row.shape)
    others = shift(pieces, "core", 2, 1)
    half = project(True, place, tokens, pieces, fsdp * breadth)
    preact = project(False, place, tokens, others, fsdp * breadth, half)
    return new_momentum, preact


def solution(mesh):
    split_mesh = Mesh(mesh.devices.reshape(SIZES + mesh.devices.shape[1:]), AXES)
    dp = AXES[:4]
    return jax.shard_map(
        on_device,
        mesh=split_mesh,
        in_specs=(
            P(dp, None, "fsdp"),
            P(dp, None, "fsdp"),
            P(None, "fsdp"),
            P(dp + ("fsdp",), None),
            P(dp, None, "fsdp", None),
        ),
        out_specs=(P(dp, None, "fsdp"), P(dp + ("fsdp",), None)),
        check_vma=False,
    )
```

```python
import jax
import jax.numpy as jnp
import ml_dtypes
import numpy as np
from jax import lax
from jax.experimental import pallas as pl
from jax.experimental.pallas import tpu as pltpu
from jax.sharding import Mesh
from jax.sharding import PartitionSpec as P

GROUP = 64
BLOCK = 8
KEEP = 4
LANES = 128
BATCHES = (0, 2, 4)
ROWS = 16
DECAY = 0.9
STEP = 5.0
F32 = jnp.float32
BF16 = jnp.bfloat16
AXES = ("x", "y", "zl", "core", "fsdp")
SIZES = (4, 4, 2, 2)


def halves(table):
    high = table.astype(ml_dtypes.bfloat16)
    low = (table - high.astype(np.float64)).astype(ml_dtypes.bfloat16)
    return high, low


def cosine_table():
    position = np.arange(GROUP, dtype=np.float64)
    frequency = position[:, None]
    factor = np.where(frequency == 0, np.sqrt(1.0 / GROUP), np.sqrt(2.0 / GROUP))
    return factor * np.cos(np.pi * (2.0 * position[None, :] + 1.0) * frequency / (2.0 * GROUP))


def left_operand(table):
    high, low = halves(table)
    return np.concatenate([high, high, low, low], axis=1)


def right_operand(table):
    high, low = halves(np.kron(np.eye(LANES // GROUP), table))
    return np.block([[high, low], [high, low]])


def split(value):
    high = value.astype(BF16)
    return high, (value - high.astype(F32)).astype(BF16)


def mix_rows(operand, value):
    high, low = split(value)
    return jnp.dot(
        operand, jnp.concatenate([high, low, high, low], axis=0), preferred_element_type=F32
    )


def mix_columns(value, operand):
    high, low = split(value)
    both = jnp.dot(
        jnp.concatenate([high, low], axis=1), operand, preferred_element_type=F32
    )
    return both[:, :LANES] + both[:, LANES:]


def whereabouts():
    x, y, core, shard = (lax.axis_index(a) for a in ("x", "y", "core", "fsdp"))
    return jnp.where(core == 0, x, y), jnp.where(core == 0, y, x), core, shard


def compress_kernel(first, tiles, steps, index, momentum, gradient, weight, *rest):
    place = whereabouts()
    operands, rest = rest[:4], rest[4:]
    if first:
        new_momentum, sent, own_weight = rest[:3]
    else:
        new_momentum, sent = rest[1:3]
    moment_buf, grad_buf, new_buf, weight_buf, *rest = rest[3:]
    tables, (in_sems, out_sems, table_sems, sent_buf, sent_sems, picked) = rest[:4], rest[4:]
    wide = tiles * LANES
    core = place[2]
    half = (1 - core) if first else core

    spans = [slice(a * wide, b * wide) for a, b in zip(BATCHES, BATCHES[1:])]

    def columns(span):
        return pl.ds(
            pl.multiple_of(half * steps * wide + span.start, LANES), span.stop - span.start
        )

    loads = [
        (
            pltpu.make_async_copy(
                momentum.at[0, :, columns(span)], moment_buf.at[:, span], in_sems.at[n, 0]
            ),
            pltpu.make_async_copy(
                gradient.at[0, :, columns(span)], grad_buf.at[:, span], in_sems.at[n, 1]
            ),
        )
        for n, span in enumerate(spans)
    ]
    table_loads = [
        pltpu.make_async_copy(operands[n], tables[n], table_sems.at[n]) for n in range(4)
    ]
    index_load = pltpu.make_async_copy(index, picked, table_sems.at[5])
    for copy in (*loads[0], index_load, *table_loads, *(copy for pair in loads[1:] for copy in pair)):
        copy.start()
    if first:
        at = pl.multiple_of((core * steps + place[1]) * wide, wide)
        row = pl.multiple_of(place[0] * ROWS, ROWS)
        weight_load = pltpu.make_async_copy(
            weight.at[pl.ds(row, ROWS), pl.ds(at, wide)], weight_buf, table_sems.at[4]
        )
        weight_load.start()
    lane = lax.broadcasted_iota(jnp.int32, (BLOCK, LANES), 1)
    lane_block = (lane % GROUP) // BLOCK
    left_group = lane < GROUP
    row_block = lax.broadcasted_iota(jnp.int32, (GROUP // BLOCK, BLOCK, LANES), 0) * BLOCK
    stores = []
    for n, span in enumerate(spans):
        for copy in loads[n]:
            copy.wait()
        if n == 0:
            for copy in (index_load, *table_loads):
                copy.wait()
        row_fwd, col_fwd, row_inv, col_inv = tables
        count = (span.stop - span.start) // LANES
        moment = DECAY * moment_buf[:, span] + grad_buf[:, span].astype(F32)
        mixed = mix_rows(row_fwd[...], moment)
        stacked = jnp.concatenate(
            [mixed[:, t * LANES : (t + 1) * LANES] for t in range(count)], axis=0
        )
        coefficients = mix_columns(stacked, col_fwd[...])
        start = half * steps * tiles * (LANES // GROUP) + span.start // GROUP
        kept = []
        for t in range(count):
            mask = None
            for k in range(KEEP):
                wanted = jnp.where(
                    left_group, picked[k, start + 2 * t], picked[k, start + 2 * t + 1]
                ) - lane_block
                hit = wanted[None] == row_block
                mask = hit if mask is None else mask | hit
            part = coefficients[t * GROUP : (t + 1) * GROUP].reshape(GROUP // BLOCK, BLOCK, LANES)
            kept.append(jnp.where(mask, part, 0.0).reshape(GROUP, LANES))
        unmixed = mix_columns(jnp.concatenate(kept, axis=0), col_inv[...])
        spread = jnp.concatenate(
            [unmixed[t * GROUP : (t + 1) * GROUP] for t in range(count)], axis=1
        )
        transmitted = mix_rows(row_inv[...], spread)
        new_buf[:, span] = moment - transmitted
        store = pltpu.make_async_copy(
            new_buf.at[:, span], new_momentum.at[0, :, columns(span)], out_sems.at[n]
        )
        store.start()
        stores.append(store)
        for j in range(span.start // wide, span.stop // wide):
            for i in range(GROUP // ROWS):
                outer = jnp.where(half == 0, i, j)
                inner = jnp.where(half == 0, j, i)
                for t in range(tiles):
                    at = j * wide + t * LANES - span.start
                    sent_buf[j, i, t] = transmitted[i * ROWS : (i + 1) * ROWS, at : at + LANES]
                store = pltpu.make_async_copy(
                    sent_buf.at[j, i], sent.at[outer, inner], sent_sems.at[j, i]
                )
                store.start()
                stores.append(store)
    if first:
        weight_load.wait()
        for t in range(tiles):
            own_weight[t] = weight_buf[:, t * LANES : (t + 1) * LANES].astype(F32)
    for store in stores:
        store.wait()


def compress(first, picked, momentum, gradient, weight, tables, partial=None):
    height, breadth = weight.shape
    steps = SIZES[1]
    wide = breadth // 2 // steps
    tiles = wide // LANES
    chunk = (tiles, ROWS, LANES)
    in_specs = [pl.BlockSpec(memory_space=pltpu.HBM)] * (4 + len(tables))
    out_shape = [
        jax.ShapeDtypeStruct((1, height, breadth), F32),
        jax.ShapeDtypeStruct((SIZES[0], steps) + chunk, F32),
    ]
    out_specs = [pl.BlockSpec(memory_space=pltpu.HBM)] * 2
    operands = [picked, momentum, gradient, weight, *tables]
    aliases = {}
    if first:
        out_shape.append(jax.ShapeDtypeStruct(chunk, F32))
        out_specs.append(pl.BlockSpec(memory_space=pltpu.VMEM))
    else:
        aliases = {len(operands): 0}
        operands.append(partial)
        in_specs.append(pl.BlockSpec(memory_space=pltpu.HBM))

    def body(*refs):
        compress_kernel(first, tiles, steps, *refs)

    return pl.pallas_call(
        body,
        in_specs=in_specs,
        out_specs=out_specs,
        out_shape=out_shape,
        scratch_shapes=[
            pltpu.VMEM((height, steps * wide), F32),
            pltpu.VMEM((height, steps * wide), BF16),
            pltpu.VMEM((height, steps * wide), F32),
            pltpu.VMEM((ROWS, wide), BF16),
            *(pltpu.VMEM(table.shape, BF16) for table in tables),
            pltpu.SemaphoreType.DMA((steps, 2)),
            pltpu.SemaphoreType.DMA((steps,)),
            pltpu.SemaphoreType.DMA((6,)),
            pltpu.VMEM((steps, SIZES[0]) + chunk, F32),
            pltpu.SemaphoreType.DMA((steps, SIZES[0])),
            pltpu.SMEM(picked.shape, jnp.int32),
        ],
        input_output_aliases=aliases,
        compiler_params=pltpu.CompilerParams(vmem_limit_bytes=60 * 2**20),
        cost_estimate=pl.CostEstimate(
            flops=2 * 4 * 256 * height * breadth, bytes_accessed=6 * height * breadth, transcendentals=0
        ),
        name="compress_first" if first else "compress_second",
    )(*operands)


def project(tokens, pieces, own, steps, shards, breadth, partial=None):
    count, depth = tokens.shape
    _, side, tiles, rows, lanes = pieces[0].shape
    wide = tiles * lanes
    number = len(pieces)
    slots = sum(len(held) for held in shards)

    def body(tokens, *rest):
        place = whereabouts()
        arrays, (out, held, sems) = rest[:number], rest[-3:]
        turn_of, start = (place[0], place[1]) if own else (place[1], place[0])
        half = place[2] if own else 1 - place[2]
        order = [lax.rem(turn_of - i + side, side) for i in range(side)]
        copies = []
        for n in range(number):
            at = half * side + lax.rem(start - steps[n] + side, side)
            for k, shard in enumerate(shards[n]):
                slot = len(copies)
                table = jnp.concatenate(
                    [
                        jnp.concatenate([arrays[n][k, order[i], t] for i in range(side)], axis=0)
                        for t in range(tiles)
                    ],
                    axis=1,
                )
                held[slot] = jnp.dot(
                    tokens[...], table, preferred_element_type=F32
                ).astype(BF16)
                column = pl.multiple_of(((place[3] ^ shard) * 2 * side + at) * wide, wide)
                copy = pltpu.make_async_copy(
                    held.at[slot], out.at[:, pl.ds(column, wide)], sems.at[slot]
                )
                copy.start()
                copies.append(copy)
        for copy in copies:
            copy.wait()

    operands = [tokens, *pieces]
    in_specs = [pl.BlockSpec(memory_space=pltpu.VMEM)] * (1 + number)
    aliases = {}
    if partial is not None:
        aliases = {len(operands): 0}
        operands.append(partial)
        in_specs.append(pl.BlockSpec(memory_space=pltpu.HBM))
    return pl.pallas_call(
        body,
        in_specs=in_specs,
        out_specs=pl.BlockSpec(memory_space=pltpu.HBM),
        out_shape=jax.ShapeDtypeStruct((count, breadth), BF16),
        scratch_shapes=[
            pltpu.VMEM((slots, count, wide), BF16),
            pltpu.SemaphoreType.DMA((slots,)),
        ],
        input_output_aliases=aliases,
        compiler_params=pltpu.CompilerParams(vmem_limit_bytes=16 * 2**20),
        cost_estimate=pl.CostEstimate(
            flops=2 * count * depth * wide * slots,
            bytes_accessed=30 * 2**20 * number,
            transcendentals=0,
        ),
        name="project",
    )(*operands)


def after(preact, *values):
    def body(*refs):
        pass

    spaces = [pltpu.VMEM] * len(values) + [pltpu.HBM]
    operands = (*values, preact)
    return pl.pallas_call(
        body,
        in_specs=[pl.BlockSpec(memory_space=space) for space in spaces],
        out_specs=[pl.BlockSpec(memory_space=space) for space in spaces],
        out_shape=[jax.ShapeDtypeStruct(v.shape, v.dtype) for v in operands],
        input_output_aliases={n: n for n in range(len(operands))},
        compiler_params=pltpu.CompilerParams(vmem_limit_bytes=16 * 2**20),
        name="after",
    )(*operands)


def shift(value, axis, size, by):
    return lax.ppermute(value, axis, [(i, (i + by) % size) for i in range(size)])


def flip(value, axis, size, mask):
    return lax.ppermute(value, axis, [(i, i ^ mask) for i in range(size)])


def turn(value, by, late):
    rows, cols, _, cores = SIZES
    pairs = []
    for x in range(rows):
        for y in range(cols):
            for core in range(cores):
                along_x = (core == 0) != late
                there = ((x + by) % rows, y) if along_x else (x, (y + by) % cols)
                pairs.append(((x * cols + y) * cores + core, (there[0] * cols + there[1]) * cores + core))
    return lax.ppermute(value, ("x", "y", "core"), pairs)


def on_device(momentum, gradient, weight, tokens, block_index):
    fsdp = lax.axis_size("fsdp")
    side = SIZES[0]
    plane = side * side
    full = fsdp * weight.shape[1]
    picked = block_index[0, 0].T
    cosines = cosine_table()
    tables = [
        jnp.asarray(left_operand(cosines)),
        jnp.asarray(right_operand(cosines.T)),
        jnp.asarray(left_operand(cosines.T)),
        jnp.asarray(right_operand(cosines)),
    ]
    partial, away, own_weight = compress(True, picked, momentum, gradient, weight, tables)
    arrived = shift(away, "core", 2, 1)
    new_momentum, kept = compress(
        False, picked, momentum, gradient, weight, tables, partial
    )
    pair = (kept + arrived).astype(BF16)
    pair = pair.reshape((plane,) + pair.shape[2:])
    parts = lax.all_to_all(pair, ("x", "y"), 0, 0, tiled=True)
    summed = jnp.sum(parts.astype(F32), axis=0)
    total = summed + shift(summed, "zl", 2, 1)
    replicas = float(np.prod(SIZES))
    chunk = (own_weight - (STEP / replicas) * total).astype(BF16)
    row = jnp.stack([chunk] + [flip(chunk, "fsdp", fsdp, k) for k in range(1, fsdp)])
    stack = jnp.stack([row] + [turn(row, d, False) for d in range(1, side)], axis=1)
    every = tuple(range(fsdp))
    lower, upper = every[: fsdp // 2], every[fsdp // 2 :]
    swap = lambda value: shift(value, "core", 2, 1)

    def run(arrays, steps, shards, preact):
        return project(tokens, arrays, True, steps, shards, full, preact)

    def run_other(arrays, steps, shards, preact):
        return project(tokens, arrays, False, steps, shards, full, preact)

    other = swap(stack)
    left, right = turn(stack, 1, True), turn(stack, 3, True)
    preact = run([stack], (0,), (every,), None)
    preact = run_other([other], (0,), (every,), preact)
    left, right, preact = after(preact, left, right)
    far = [turn(left[: fsdp // 2], 1, True), turn(right[fsdp // 2 :], 3, True)]
    others = [swap(left), swap(right)]
    preact = run([left, right], (1, 3), (every, every), preact)
    preact = run_other(others, (1, 3), (every, every), preact)
    *far, preact = after(preact, *far)
    others = [swap(value) for value in far]
    preact = run(far, (2, 2), (lower, upper), preact)
    preact = run_other(others, (2, 2), (lower, upper), preact)
    return new_momentum, preact


def solution(mesh):
    split_mesh = Mesh(mesh.devices.reshape(SIZES + mesh.devices.shape[1:]), AXES)
    dp = AXES[:4]
    return jax.shard_map(
        on_device,
        mesh=split_mesh,
        in_specs=(
            P(dp, None, "fsdp"),
            P(dp, None, "fsdp"),
            P(None, "fsdp"),
            P(dp + ("fsdp",), None),
            P(dp, None, "fsdp", None),
        ),
        out_specs=(P(dp, None, "fsdp"), P(dp + ("fsdp",), None)),
        check_vma=False,
    )
```

```python
import jax
import jax.numpy as jnp
import ml_dtypes
import numpy as np
from jax import lax
from jax.experimental import pallas as pl
from jax.experimental.pallas import tpu as pltpu
from jax.sharding import Mesh
from jax.sharding import PartitionSpec as P

GROUP = 64
BLOCK = 8
KEEP = 4
LANES = 128
BATCHES = (0, 2, 4)
ROWS = 16
DECAY = 0.9
STEP = 5.0
F32 = jnp.float32
BF16 = jnp.bfloat16
AXES = ("x", "y", "zl", "core", "fsdp")
SIZES = (4, 4, 2, 2)


def halves(table):
    high = table.astype(ml_dtypes.bfloat16)
    low = (table - high.astype(np.float64)).astype(ml_dtypes.bfloat16)
    return high, low


def cosine_table():
    position = np.arange(GROUP, dtype=np.float64)
    frequency = position[:, None]
    factor = np.where(frequency == 0, np.sqrt(1.0 / GROUP), np.sqrt(2.0 / GROUP))
    return factor * np.cos(np.pi * (2.0 * position[None, :] + 1.0) * frequency / (2.0 * GROUP))


def left_operand(table):
    high, low = halves(table)
    return np.concatenate([high, high, low, low], axis=1)


def right_operand(table):
    high, low = halves(np.kron(np.eye(LANES // GROUP), table))
    return np.block([[high, low], [high, low]])


def split(value):
    high = value.astype(BF16)
    return high, (value - high.astype(F32)).astype(BF16)


def mix_rows(operand, value):
    high, low = split(value)
    return jnp.dot(
        operand, jnp.concatenate([high, low, high, low], axis=0), preferred_element_type=F32
    )


def mix_columns(value, operand):
    high, low = split(value)
    both = jnp.dot(
        jnp.concatenate([high, low], axis=1), operand, preferred_element_type=F32
    )
    return both[:, :LANES] + both[:, LANES:]


def whereabouts():
    x, y, low, core, shard = (lax.axis_index(a) for a in AXES)
    return jnp.where(core == 0, x, y), jnp.where(core == 0, y, x), low, core, shard


def chunk_column(second, low):
    return lax.rem(second + 2 * low, SIZES[1])


def compress_kernel(first, tiles, steps, index, momentum, gradient, weight, *rest):
    place = whereabouts()
    operands, rest = rest[:4], rest[4:]
    if first:
        new_momentum, sent, own_weight = rest[:3]
    else:
        new_momentum, sent = rest[1:3]
    moment_buf, grad_buf, new_buf, weight_buf, *rest = rest[3:]
    tables, (in_sems, out_sems, table_sems, sent_buf, sent_sems, picked) = rest[:4], rest[4:]
    wide = tiles * LANES
    first_axis, second_axis, low, core = place[:4]
    half = (1 - core) if first else core

    spans = [slice(a * wide, b * wide) for a, b in zip(BATCHES, BATCHES[1:])]

    def columns(span):
        return pl.ds(
            pl.multiple_of(half * steps * wide + span.start, LANES), span.stop - span.start
        )

    loads = [
        (
            pltpu.make_async_copy(
                momentum.at[0, :, columns(span)], moment_buf.at[:, span], in_sems.at[n, 0]
            ),
            pltpu.make_async_copy(
                gradient.at[0, :, columns(span)], grad_buf.at[:, span], in_sems.at[n, 1]
            ),
        )
        for n, span in enumerate(spans)
    ]
    table_loads = [
        pltpu.make_async_copy(operands[n], tables[n], table_sems.at[n]) for n in range(4)
    ]
    index_load = pltpu.make_async_copy(index, picked, table_sems.at[5])
    for copy in (*loads[0], index_load, *table_loads, *(copy for pair in loads[1:] for copy in pair)):
        copy.start()
    if first:
        at = pl.multiple_of((core * steps + chunk_column(second_axis, low)) * wide, wide)
        row = pl.multiple_of(first_axis * ROWS, ROWS)
        weight_load = pltpu.make_async_copy(
            weight.at[pl.ds(row, ROWS), pl.ds(at, wide)], weight_buf, table_sems.at[4]
        )
        weight_load.start()
    lane = lax.broadcasted_iota(jnp.int32, (BLOCK, LANES), 1)
    lane_block = (lane % GROUP) // BLOCK
    left_group = lane < GROUP
    row_block = lax.broadcasted_iota(jnp.int32, (GROUP // BLOCK, BLOCK, LANES), 0) * BLOCK
    stores = []
    for n, span in enumerate(spans):
        for copy in loads[n]:
            copy.wait()
        if n == 0:
            for copy in (index_load, *table_loads):
                copy.wait()
        row_fwd, col_fwd, row_inv, col_inv = tables
        count = (span.stop - span.start) // LANES
        moment = DECAY * moment_buf[:, span] + grad_buf[:, span].astype(F32)
        mixed = mix_rows(row_fwd[...], moment)
        stacked = jnp.concatenate(
            [mixed[:, t * LANES : (t + 1) * LANES] for t in range(count)], axis=0
        )
        coefficients = mix_columns(stacked, col_fwd[...])
        start = half * steps * tiles * (LANES // GROUP) + span.start // GROUP
        kept = []
        for t in range(count):
            mask = None
            for k in range(KEEP):
                wanted = jnp.where(
                    left_group, picked[k, start + 2 * t], picked[k, start + 2 * t + 1]
                ) - lane_block
                hit = wanted[None] == row_block
                mask = hit if mask is None else mask | hit
            part = coefficients[t * GROUP : (t + 1) * GROUP].reshape(GROUP // BLOCK, BLOCK, LANES)
            kept.append(jnp.where(mask, part, 0.0).reshape(GROUP, LANES))
        unmixed = mix_columns(jnp.concatenate(kept, axis=0), col_inv[...])
        spread = jnp.concatenate(
            [unmixed[t * GROUP : (t + 1) * GROUP] for t in range(count)], axis=1
        )
        transmitted = mix_rows(row_inv[...], spread)
        new_buf[:, span] = moment - transmitted
        store = pltpu.make_async_copy(
            new_buf.at[:, span], new_momentum.at[0, :, columns(span)], out_sems.at[n]
        )
        store.start()
        stores.append(store)
        for j in range(span.start // wide, span.stop // wide):
            for i in range(GROUP // ROWS):
                goal = chunk_column(j, low)
                outer = jnp.where(half == 0, i, goal)
                inner = jnp.where(half == 0, goal, i)
                for t in range(tiles):
                    at = j * wide + t * LANES - span.start
                    sent_buf[j, i, t] = transmitted[i * ROWS : (i + 1) * ROWS, at : at + LANES]
                store = pltpu.make_async_copy(
                    sent_buf.at[j, i], sent.at[outer, inner], sent_sems.at[j, i]
                )
                store.start()
                stores.append(store)
    if first:
        weight_load.wait()
        for t in range(tiles):
            own_weight[t] = weight_buf[:, t * LANES : (t + 1) * LANES].astype(F32)
    for store in stores:
        store.wait()


def compress(first, picked, momentum, gradient, weight, tables, partial=None):
    height, breadth = weight.shape
    steps = SIZES[1]
    wide = breadth // 2 // steps
    tiles = wide // LANES
    chunk = (tiles, ROWS, LANES)
    in_specs = [pl.BlockSpec(memory_space=pltpu.HBM)] * (4 + len(tables))
    out_shape = [
        jax.ShapeDtypeStruct((1, height, breadth), F32),
        jax.ShapeDtypeStruct((SIZES[0], steps) + chunk, F32),
    ]
    out_specs = [pl.BlockSpec(memory_space=pltpu.HBM)] * 2
    operands = [picked, momentum, gradient, weight, *tables]
    aliases = {}
    if first:
        out_shape.append(jax.ShapeDtypeStruct(chunk, F32))
        out_specs.append(pl.BlockSpec(memory_space=pltpu.VMEM))
    else:
        aliases = {len(operands): 0}
        operands.append(partial)
        in_specs.append(pl.BlockSpec(memory_space=pltpu.HBM))

    def body(*refs):
        compress_kernel(first, tiles, steps, *refs)

    return pl.pallas_call(
        body,
        in_specs=in_specs,
        out_specs=out_specs,
        out_shape=out_shape,
        scratch_shapes=[
            pltpu.VMEM((height, steps * wide), F32),
            pltpu.VMEM((height, steps * wide), BF16),
            pltpu.VMEM((height, steps * wide), F32),
            pltpu.VMEM((ROWS, wide), BF16),
            *(pltpu.VMEM(table.shape, BF16) for table in tables),
            pltpu.SemaphoreType.DMA((steps, 2)),
            pltpu.SemaphoreType.DMA((steps,)),
            pltpu.SemaphoreType.DMA((6,)),
            pltpu.VMEM((steps, SIZES[0]) + chunk, F32),
            pltpu.SemaphoreType.DMA((steps, SIZES[0])),
            pltpu.SMEM(picked.shape, jnp.int32),
        ],
        input_output_aliases=aliases,
        compiler_params=pltpu.CompilerParams(vmem_limit_bytes=60 * 2**20),
        cost_estimate=pl.CostEstimate(
            flops=2 * 4 * 256 * height * breadth, bytes_accessed=6 * height * breadth, transcendentals=0
        ),
        name="compress_first" if first else "compress_second",
    )(*operands)


def row_shard(shard, low, k):
    return shard ^ k


def below_shard(shard, low, k):
    return 2 + (((shard + 1 - low) & 1) ^ k)


def above_shard(shard, low, k):
    return ((shard + low) & 1) ^ k


def project(tokens, pieces, own, steps, shards, breadth, partial=None):
    count, depth = tokens.shape
    _, side, tiles, rows, lanes = pieces[0].shape
    wide = tiles * lanes
    number = len(pieces)
    slots = sum(piece.shape[0] for piece in pieces)

    def body(tokens, *rest):
        place = whereabouts()
        arrays, (out, held, sems) = rest[:number], rest[-3:]
        first, second, low, core, mine = place
        turn_of, start = (first, second) if own else (second, first)
        start = chunk_column(start, low)
        half = core if own else 1 - core
        order = [lax.rem(turn_of - i + side, side) for i in range(side)]
        copies = []
        for n in range(number):
            at = half * side + lax.rem(start - steps[n] + side, side)
            for k in range(pieces[n].shape[0]):
                slot = len(copies)
                table = jnp.concatenate(
                    [
                        jnp.concatenate([arrays[n][k, order[i], t] for i in range(side)], axis=0)
                        for t in range(tiles)
                    ],
                    axis=1,
                )
                held[slot] = jnp.dot(
                    tokens[...], table, preferred_element_type=F32
                ).astype(BF16)
                column = pl.multiple_of((shards[n](mine, low, k) * 2 * side + at) * wide, wide)
                copy = pltpu.make_async_copy(
                    held.at[slot], out.at[:, pl.ds(column, wide)], sems.at[slot]
                )
                copy.start()
                copies.append(copy)
        for copy in copies:
            copy.wait()

    operands = [tokens, *pieces]
    in_specs = [pl.BlockSpec(memory_space=pltpu.VMEM)] * (1 + number)
    aliases = {}
    if partial is not None:
        aliases = {len(operands): 0}
        operands.append(partial)
        in_specs.append(pl.BlockSpec(memory_space=pltpu.HBM))
    return pl.pallas_call(
        body,
        in_specs=in_specs,
        out_specs=pl.BlockSpec(memory_space=pltpu.HBM),
        out_shape=jax.ShapeDtypeStruct((count, breadth), BF16),
        scratch_shapes=[
            pltpu.VMEM((slots, count, wide), BF16),
            pltpu.SemaphoreType.DMA((slots,)),
        ],
        input_output_aliases=aliases,
        compiler_params=pltpu.CompilerParams(vmem_limit_bytes=16 * 2**20),
        cost_estimate=pl.CostEstimate(
            flops=2 * count * depth * wide * slots,
            bytes_accessed=4 * count * wide * slots,
            transcendentals=0,
        ),
        name="project",
    )(*operands)


def after(preact, *values):
    def body(*refs):
        pass

    spaces = [pltpu.VMEM] * len(values) + [pltpu.HBM]
    operands = (*values, preact)
    return pl.pallas_call(
        body,
        in_specs=[pl.BlockSpec(memory_space=space) for space in spaces],
        out_specs=[pl.BlockSpec(memory_space=space) for space in spaces],
        out_shape=[jax.ShapeDtypeStruct(v.shape, v.dtype) for v in operands],
        input_output_aliases={n: n for n in range(len(operands))},
        compiler_params=pltpu.CompilerParams(vmem_limit_bytes=16 * 2**20),
        name="after",
    )(*operands)


def move(value, goal, *axes):
    extent = [lax.axis_size(axis) for axis in axes]
    places = list(np.ndindex(*extent))
    number = {spot: n for n, spot in enumerate(places)}
    pairs = []
    for spot in places:
        there = tuple(c % e for c, e in zip(goal(*spot), extent))
        pairs.append((number[spot], number[there]))
    return lax.ppermute(value, axes, pairs)


def swap(value):
    return move(value, lambda core: (core + 1,), "core")


def flip(value, mask):
    return move(value, lambda shard: (shard ^ mask,), "fsdp")


def turn(value, by, late):
    def goal(x, y, core):
        return (x + by, y, core) if (core == 0) != late else (x, y + by, core)

    return move(value, goal, "x", "y", "core")


def across(value):
    def goal(x, y, low, core):
        return (x, y + 2, low + 1, core) if core == 0 else (x + 2, y, low + 1, core)

    return move(value, goal, "x", "y", "zl", "core")


def climb(value, by):
    def goal(low, shard):
        z = 2 * shard + low + by
        return z % 2, z // 2

    return move(value, goal, "zl", "fsdp")


def on_device(momentum, gradient, weight, tokens, block_index):
    fsdp = lax.axis_size("fsdp")
    side = SIZES[0]
    plane = side * side
    full = fsdp * weight.shape[1]
    picked = block_index[0, 0].T
    cosines = cosine_table()
    tables = [
        jnp.asarray(left_operand(cosines)),
        jnp.asarray(right_operand(cosines.T)),
        jnp.asarray(left_operand(cosines.T)),
        jnp.asarray(right_operand(cosines)),
    ]
    partial, away, own_weight = compress(True, picked, momentum, gradient, weight, tables)
    arrived = swap(away)
    new_momentum, kept = compress(
        False, picked, momentum, gradient, weight, tables, partial
    )
    pair = (kept + arrived).astype(BF16)
    pair = pair.reshape((plane,) + pair.shape[2:])
    parts = lax.all_to_all(pair, ("x", "y"), 0, 0, tiled=True)
    summed = jnp.sum(parts.astype(F32), axis=0)
    total = summed + across(summed)
    replicas = float(np.prod(SIZES))
    chunk = (own_weight - (STEP / replicas) * total).astype(BF16)
    row = jnp.stack([chunk] + [flip(chunk, k) for k in range(1, fsdp)])
    stack = jnp.stack([row] + [turn(row, d, False) for d in range(1, side)], axis=1)
    left, right = turn(stack, 1, True), turn(stack, 3, True)
    near_half, far_half = stack[: fsdp // 2], stack[fsdp // 2 :]
    low_shards = lax.axis_index("fsdp") < fsdp // 2
    below = climb(jnp.where(low_shards, far_half, near_half), 1)
    above = climb(jnp.where(low_shards, near_half, far_half), -1)
    preact = project(tokens, [stack], True, (0,), (row_shard,), full)
    *arrays, preact = after(preact, stack, left, right, below, above)
    others = [swap(value) for value in arrays]
    steps = (0, 1, 3, 2, 2)
    shards = (row_shard, row_shard, row_shard, below_shard, above_shard)
    preact = project(tokens, arrays[1:], True, steps[1:], shards[1:], full, preact)
    preact = project(tokens, others, False, steps, shards, full, preact)
    return new_momentum, preact


def solution(mesh):
    split_mesh = Mesh(mesh.devices.reshape(SIZES + mesh.devices.shape[1:]), AXES)
    dp = AXES[:4]
    return jax.shard_map(
        on_device,
        mesh=split_mesh,
        in_specs=(
            P(dp, None, "fsdp"),
            P(dp, None, "fsdp"),
            P(None, "fsdp"),
            P(dp + ("fsdp",), None),
            P(dp, None, "fsdp", None),
        ),
        out_specs=(P(dp, None, "fsdp"), P(dp + ("fsdp",), None)),
        check_vma=False,
    )
```

```python
import jax
import jax.numpy as jnp
import ml_dtypes
import numpy as np
from jax import lax
from jax.experimental import pallas as pl
from jax.experimental.pallas import tpu as pltpu
from jax.sharding import Mesh
from jax.sharding import PartitionSpec as P

GROUP = 64
BLOCK = 8
KEEP = 4
LANES = 128
BATCHES = (0, 2, 4)
ROWS = 16
DECAY = 0.9
STEP = 5.0
F32 = jnp.float32
BF16 = jnp.bfloat16
AXES = ("x", "y", "zl", "core", "fsdp")
SIZES = (4, 4, 2, 2)


def halves(table):
    high = table.astype(ml_dtypes.bfloat16)
    low = (table - high.astype(np.float64)).astype(ml_dtypes.bfloat16)
    return high, low


def cosine_table():
    position = np.arange(GROUP, dtype=np.float64)
    frequency = position[:, None]
    factor = np.where(frequency == 0, np.sqrt(1.0 / GROUP), np.sqrt(2.0 / GROUP))
    return factor * np.cos(np.pi * (2.0 * position[None, :] + 1.0) * frequency / (2.0 * GROUP))


def left_operand(table):
    high, low = halves(table)
    return np.concatenate([high, high, low, low], axis=1)


def right_operand(table):
    high, low = halves(np.kron(np.eye(LANES // GROUP), table))
    return np.block([[high, low], [high, low]])


def split(value):
    high = value.astype(BF16)
    return high, (value - high.astype(F32)).astype(BF16)


def mix_rows(operand, value):
    high, low = split(value)
    return jnp.dot(
        operand, jnp.concatenate([high, low, high, low], axis=0), preferred_element_type=F32
    )


def mix_columns(value, operand):
    high, low = split(value)
    both = jnp.dot(
        jnp.concatenate([high, low], axis=1), operand, preferred_element_type=F32
    )
    return both[:, :LANES] + both[:, LANES:]


def whereabouts():
    x, y, low, core, shard = (lax.axis_index(a) for a in AXES)
    return jnp.where(core == 0, x, y), jnp.where(core == 0, y, x), low, core, shard


def chunk_column(second, low):
    return lax.rem(second + 2 * low, SIZES[1])


def compress_kernel(first, tiles, steps, index, momentum, gradient, *rest):
    place = whereabouts()
    operands, rest = rest[:4], rest[4:]
    rest = rest if first else rest[1:]
    new_momentum, sent, moment_buf, grad_buf, new_buf, *rest = rest
    tables, (in_sems, out_sems, table_sems, sent_buf, sent_sems, picked) = rest[:4], rest[4:]
    wide = tiles * LANES
    low, core = place[2:4]
    half = (1 - core) if first else core

    spans = [slice(a * wide, b * wide) for a, b in zip(BATCHES, BATCHES[1:])]

    def columns(span):
        return pl.ds(
            pl.multiple_of(half * steps * wide + span.start, LANES), span.stop - span.start
        )

    loads = [
        (
            pltpu.make_async_copy(
                momentum.at[0, :, columns(span)], moment_buf.at[:, span], in_sems.at[n, 0]
            ),
            pltpu.make_async_copy(
                gradient.at[0, :, columns(span)], grad_buf.at[:, span], in_sems.at[n, 1]
            ),
        )
        for n, span in enumerate(spans)
    ]
    table_loads = [
        pltpu.make_async_copy(operands[n], tables[n], table_sems.at[n]) for n in range(4)
    ]
    index_load = pltpu.make_async_copy(index, picked, table_sems.at[4])
    for copy in (*loads[0], index_load, *table_loads, *(copy for pair in loads[1:] for copy in pair)):
        copy.start()
    lane = lax.broadcasted_iota(jnp.int32, (BLOCK, LANES), 1)
    lane_block = (lane % GROUP) // BLOCK
    left_group = lane < GROUP
    row_block = lax.broadcasted_iota(jnp.int32, (GROUP // BLOCK, BLOCK, LANES), 0) * BLOCK
    stores = []
    for n, span in enumerate(spans):
        for copy in loads[n]:
            copy.wait()
        if n == 0:
            for copy in (index_load, *table_loads):
                copy.wait()
        row_fwd, col_fwd, row_inv, col_inv = tables
        count = (span.stop - span.start) // LANES
        moment = DECAY * moment_buf[:, span] + grad_buf[:, span].astype(F32)
        mixed = mix_rows(row_fwd[...], moment)
        stacked = jnp.concatenate(
            [mixed[:, t * LANES : (t + 1) * LANES] for t in range(count)], axis=0
        )
        coefficients = mix_columns(stacked, col_fwd[...])
        start = half * steps * tiles * (LANES // GROUP) + span.start // GROUP
        kept = []
        for t in range(count):
            mask = None
            for k in range(KEEP):
                wanted = jnp.where(
                    left_group, picked[k, start + 2 * t], picked[k, start + 2 * t + 1]
                ) - lane_block
                hit = wanted[None] == row_block
                mask = hit if mask is None else mask | hit
            part = coefficients[t * GROUP : (t + 1) * GROUP].reshape(GROUP // BLOCK, BLOCK, LANES)
            kept.append(jnp.where(mask, part, 0.0).reshape(GROUP, LANES))
        unmixed = mix_columns(jnp.concatenate(kept, axis=0), col_inv[...])
        spread = jnp.concatenate(
            [unmixed[t * GROUP : (t + 1) * GROUP] for t in range(count)], axis=1
        )
        transmitted = mix_rows(row_inv[...], spread)
        new_buf[:, span] = moment - transmitted
        store = pltpu.make_async_copy(
            new_buf.at[:, span], new_momentum.at[0, :, columns(span)], out_sems.at[n]
        )
        store.start()
        stores.append(store)
        for j in range(span.start // wide, span.stop // wide):
            for i in range(GROUP // ROWS):
                goal = chunk_column(j, low)
                outer = jnp.where(half == 0, i, goal)
                inner = jnp.where(half == 0, goal, i)
                for t in range(tiles):
                    at = j * wide + t * LANES - span.start
                    sent_buf[j, i, t] = transmitted[i * ROWS : (i + 1) * ROWS, at : at + LANES]
                store = pltpu.make_async_copy(
                    sent_buf.at[j, i], sent.at[outer, inner], sent_sems.at[j, i]
                )
                store.start()
                stores.append(store)
    for store in stores:
        store.wait()


def compress(first, picked, momentum, gradient, tables, partial=None):
    _, height, breadth = momentum.shape
    steps = SIZES[1]
    wide = breadth // 2 // steps
    tiles = wide // LANES
    chunk = (tiles, ROWS, LANES)
    in_specs = [pl.BlockSpec(memory_space=pltpu.HBM)] * (3 + len(tables))
    out_shape = [
        jax.ShapeDtypeStruct((1, height, breadth), F32),
        jax.ShapeDtypeStruct((SIZES[0], steps) + chunk, F32),
    ]
    out_specs = [pl.BlockSpec(memory_space=pltpu.HBM)] * 2
    operands = [picked, momentum, gradient, *tables]
    aliases = {}
    if not first:
        aliases = {len(operands): 0}
        operands.append(partial)
        in_specs.append(pl.BlockSpec(memory_space=pltpu.HBM))

    def body(*refs):
        compress_kernel(first, tiles, steps, *refs)

    return pl.pallas_call(
        body,
        in_specs=in_specs,
        out_specs=out_specs,
        out_shape=out_shape,
        scratch_shapes=[
            pltpu.VMEM((height, steps * wide), F32),
            pltpu.VMEM((height, steps * wide), BF16),
            pltpu.VMEM((height, steps * wide), F32),
            *(pltpu.VMEM(table.shape, BF16) for table in tables),
            pltpu.SemaphoreType.DMA((steps, 2)),
            pltpu.SemaphoreType.DMA((steps,)),
            pltpu.SemaphoreType.DMA((5,)),
            pltpu.VMEM((steps, SIZES[0]) + chunk, F32),
            pltpu.SemaphoreType.DMA((steps, SIZES[0])),
            pltpu.SMEM(picked.shape, jnp.int32),
        ],
        input_output_aliases=aliases,
        compiler_params=pltpu.CompilerParams(vmem_limit_bytes=60 * 2**20),
        cost_estimate=pl.CostEstimate(
            flops=2 * 4 * 256 * height * breadth, bytes_accessed=6 * height * breadth, transcendentals=0
        ),
        name="compress_first" if first else "compress_second",
    )(*operands)


def row_shard(shard, low, k):
    return shard ^ k


def below_shard(shard, low, k):
    return 2 + (((shard + 1 - low) & 1) ^ k)


def above_shard(shard, low, k):
    return ((shard + low) & 1) ^ k


def own_part(weight, summed, scale):
    tiles, rows, lanes = summed.shape
    wide = tiles * lanes

    def body(weight, summed, out, held, sem):
        first, second, low, core = whereabouts()[:4]
        row = pl.multiple_of(first * rows, rows)
        at = pl.multiple_of((core * SIZES[1] + chunk_column(second, low)) * wide, wide)
        load = pltpu.make_async_copy(weight.at[pl.ds(row, rows), pl.ds(at, wide)], held, sem)
        load.start()
        load.wait()
        for t in range(tiles):
            own = held[:, t * lanes : (t + 1) * lanes].astype(F32)
            out[t] = own - scale * summed[t]

    return pl.pallas_call(
        body,
        in_specs=[pl.BlockSpec(memory_space=pltpu.HBM), pl.BlockSpec(memory_space=pltpu.VMEM)],
        out_specs=pl.BlockSpec(memory_space=pltpu.VMEM),
        out_shape=jax.ShapeDtypeStruct(summed.shape, F32),
        scratch_shapes=[pltpu.VMEM((rows, wide), BF16), pltpu.SemaphoreType.DMA],
        compiler_params=pltpu.CompilerParams(vmem_limit_bytes=16 * 2**20),
        name="own_part",
    )(weight, summed)


def project(tokens, pieces, own, steps, shards, breadth, partial=None):
    count, depth = tokens.shape
    _, side, tiles, rows, lanes = pieces[0].shape
    wide = tiles * lanes
    number = len(pieces)
    slots = sum(piece.shape[0] for piece in pieces)

    def body(tokens, *rest):
        place = whereabouts()
        arrays, (out, held, sems) = rest[:number], rest[-3:]
        first, second, low, core, mine = place
        turn_of, start = (first, second) if own else (second, first)
        start = chunk_column(start, low)
        half = core if own else 1 - core
        order = [lax.rem(turn_of - i + side, side) for i in range(side)]
        copies = []
        for n in range(number):
            at = half * side + lax.rem(start - steps[n] + side, side)
            for k in range(pieces[n].shape[0]):
                slot = len(copies)
                table = jnp.concatenate(
                    [
                        jnp.concatenate([arrays[n][k, order[i], t] for i in range(side)], axis=0)
                        for t in range(tiles)
                    ],
                    axis=1,
                )
                held[slot] = jnp.dot(
                    tokens[...], table, preferred_element_type=F32
                ).astype(BF16)
                column = pl.multiple_of((shards[n](mine, low, k) * 2 * side + at) * wide, wide)
                copy = pltpu.make_async_copy(
                    held.at[slot], out.at[:, pl.ds(column, wide)], sems.at[slot]
                )
                copy.start()
                copies.append(copy)
        for copy in copies:
            copy.wait()

    operands = [tokens, *pieces]
    in_specs = [pl.BlockSpec(memory_space=pltpu.VMEM)] * (1 + number)
    aliases = {}
    if partial is not None:
        aliases = {len(operands): 0}
        operands.append(partial)
        in_specs.append(pl.BlockSpec(memory_space=pltpu.HBM))
    return pl.pallas_call(
        body,
        in_specs=in_specs,
        out_specs=pl.BlockSpec(memory_space=pltpu.HBM),
        out_shape=jax.ShapeDtypeStruct((count, breadth), BF16),
        scratch_shapes=[
            pltpu.VMEM((slots, count, wide), BF16),
            pltpu.SemaphoreType.DMA((slots,)),
        ],
        input_output_aliases=aliases,
        compiler_params=pltpu.CompilerParams(vmem_limit_bytes=16 * 2**20),
        cost_estimate=pl.CostEstimate(
            flops=2 * count * depth * wide * slots,
            bytes_accessed=4 * count * wide * slots,
            transcendentals=0,
        ),
        name="project",
    )(*operands)


def after(preact, *values):
    def body(*refs):
        pass

    spaces = [pltpu.VMEM] * len(values) + [pltpu.HBM]
    operands = (*values, preact)
    return pl.pallas_call(
        body,
        in_specs=[pl.BlockSpec(memory_space=space) for space in spaces],
        out_specs=[pl.BlockSpec(memory_space=space) for space in spaces],
        out_shape=[jax.ShapeDtypeStruct(v.shape, v.dtype) for v in operands],
        input_output_aliases={n: n for n in range(len(operands))},
        compiler_params=pltpu.CompilerParams(vmem_limit_bytes=16 * 2**20),
        name="after",
    )(*operands)


def move(value, goal, *axes):
    extent = [lax.axis_size(axis) for axis in axes]
    places = list(np.ndindex(*extent))
    number = {spot: n for n, spot in enumerate(places)}
    pairs = []
    for spot in places:
        there = tuple(c % e for c, e in zip(goal(*spot), extent))
        pairs.append((number[spot], number[there]))
    return lax.ppermute(value, axes, pairs)


def swap(value):
    return move(value, lambda core: (core + 1,), "core")


def flip(value, mask):
    return move(value, lambda shard: (shard ^ mask,), "fsdp")


def turn(value, by, late):
    def goal(x, y, core):
        return (x + by, y, core) if (core == 0) != late else (x, y + by, core)

    return move(value, goal, "x", "y", "core")


def across(value):
    def goal(x, y, low, core):
        return (x, y + 2, low + 1, core) if core == 0 else (x + 2, y, low + 1, core)

    return move(value, goal, "x", "y", "zl", "core")


def climb(value, by):
    def goal(low, shard):
        z = 2 * shard + low + by
        return z % 2, z // 2

    return move(value, goal, "zl", "fsdp")


def on_device(momentum, gradient, weight, tokens, block_index):
    fsdp = lax.axis_size("fsdp")
    side = SIZES[0]
    plane = side * side
    full = fsdp * weight.shape[1]
    picked = block_index[0, 0].T
    cosines = cosine_table()
    tables = [
        jnp.asarray(left_operand(cosines)),
        jnp.asarray(right_operand(cosines.T)),
        jnp.asarray(left_operand(cosines.T)),
        jnp.asarray(right_operand(cosines)),
    ]
    partial, away = compress(True, picked, momentum, gradient, tables)
    arrived = swap(away)
    new_momentum, kept = compress(
        False, picked, momentum, gradient, tables, partial
    )
    pair = (kept + arrived).astype(BF16)
    pair = pair.reshape((plane,) + pair.shape[2:])
    parts = lax.all_to_all(pair, ("x", "y"), 0, 0, tiled=True)
    summed = jnp.sum(parts.astype(F32), axis=0)
    scale = STEP / float(np.prod(SIZES))
    beyond = across(summed)
    chunk = (own_part(weight, summed, scale) - scale * beyond).astype(BF16)
    row = jnp.stack([chunk] + [flip(chunk, k) for k in range(1, fsdp)])
    stack = jnp.stack([row] + [turn(row, d, False) for d in range(1, side)], axis=1)
    left, right = turn(stack, 1, True), turn(stack, 3, True)
    near_half, far_half = stack[: fsdp // 2], stack[fsdp // 2 :]
    low_shards = lax.axis_index("fsdp") < fsdp // 2
    below = climb(jnp.where(low_shards, far_half, near_half), 1)
    above = climb(jnp.where(low_shards, near_half, far_half), -1)
    preact = project(tokens, [stack], True, (0,), (row_shard,), full)
    *arrays, preact = after(preact, stack, left, right, below, above)
    others = [swap(value) for value in arrays]
    steps = (0, 1, 3, 2, 2)
    shards = (row_shard, row_shard, row_shard, below_shard, above_shard)
    preact = project(tokens, arrays[1:], True, steps[1:], shards[1:], full, preact)
    preact = project(tokens, others, False, steps, shards, full, preact)
    return new_momentum, preact


def solution(mesh):
    split_mesh = Mesh(mesh.devices.reshape(SIZES + mesh.devices.shape[1:]), AXES)
    dp = AXES[:4]
    return jax.shard_map(
        on_device,
        mesh=split_mesh,
        in_specs=(
            P(dp, None, "fsdp"),
            P(dp, None, "fsdp"),
            P(None, "fsdp"),
            P(dp + ("fsdp",), None),
            P(dp, None, "fsdp", None),
        ),
        out_specs=(P(dp, None, "fsdp"), P(dp + ("fsdp",), None)),
        check_vma=False,
    )
```

```python
import jax
import jax.numpy as jnp
import ml_dtypes
import numpy as np
from jax import lax
from jax.experimental import pallas as pl
from jax.experimental.pallas import tpu as pltpu
from jax.sharding import Mesh
from jax.sharding import PartitionSpec as P

GROUP = 64
BLOCK = 8
KEEP = 4
LANES = 128
BATCHES = (0, 2, 4)
ROWS = 16
DECAY = 0.9
STEP = 5.0
F32 = jnp.float32
BF16 = jnp.bfloat16
AXES = ("x", "y", "zl", "core", "fsdp")
SIZES = (4, 4, 2, 2)


def halves(table):
    high = table.astype(ml_dtypes.bfloat16)
    low = (table - high.astype(np.float64)).astype(ml_dtypes.bfloat16)
    return high, low


def cosine_table():
    position = np.arange(GROUP, dtype=np.float64)
    frequency = position[:, None]
    factor = np.where(frequency == 0, np.sqrt(1.0 / GROUP), np.sqrt(2.0 / GROUP))
    return factor * np.cos(np.pi * (2.0 * position[None, :] + 1.0) * frequency / (2.0 * GROUP))


def left_operand(table):
    high, low = halves(table)
    return np.concatenate([high, high, low, low], axis=1)


def right_operand(table):
    high, low = halves(np.kron(np.eye(LANES // GROUP), table))
    return np.block([[high, low], [high, low]])


def split(value):
    high = value.astype(BF16)
    return high, (value - high.astype(F32)).astype(BF16)


def mix_rows(operand, value):
    high, low = split(value)
    return jnp.dot(
        operand, jnp.concatenate([high, low, high, low], axis=0), preferred_element_type=F32
    )


def mix_columns(value, operand):
    high, low = split(value)
    both = jnp.dot(
        jnp.concatenate([high, low], axis=1), operand, preferred_element_type=F32
    )
    return both[:, :LANES] + both[:, LANES:]


def whereabouts():
    x, y, low, core, shard = (lax.axis_index(a) for a in AXES)
    return jnp.where(core == 0, x, y), jnp.where(core == 0, y, x), low, core, shard


def chunk_column(second, low):
    return lax.rem(second + 2 * low, SIZES[1])


def compress_kernel(first, tiles, steps, index, momentum, gradient, *rest):
    place = whereabouts()
    operands, rest = rest[:4], rest[4:]
    rest = rest if first else rest[1:]
    new_momentum, sent, moment_buf, grad_buf, new_buf, *rest = rest
    tables, (in_sems, out_sems, table_sems, sent_buf, sent_sems, picked) = rest[:4], rest[4:]
    wide = tiles * LANES
    low, core = place[2:4]
    half = (1 - core) if first else core

    spans = [slice(a * wide, b * wide) for a, b in zip(BATCHES, BATCHES[1:])]

    def columns(span):
        return pl.ds(
            pl.multiple_of(half * steps * wide + span.start, LANES), span.stop - span.start
        )

    loads = [
        (
            pltpu.make_async_copy(
                momentum.at[0, :, columns(span)], moment_buf.at[:, span], in_sems.at[n, 0]
            ),
            pltpu.make_async_copy(
                gradient.at[0, :, columns(span)], grad_buf.at[:, span], in_sems.at[n, 1]
            ),
        )
        for n, span in enumerate(spans)
    ]
    table_loads = [
        pltpu.make_async_copy(operands[n], tables[n], table_sems.at[n]) for n in range(4)
    ]
    index_load = pltpu.make_async_copy(index, picked, table_sems.at[4])
    for copy in (*loads[0], index_load, *table_loads, *(copy for pair in loads[1:] for copy in pair)):
        copy.start()
    lane = lax.broadcasted_iota(jnp.int32, (BLOCK, LANES), 1)
    lane_block = (lane % GROUP) // BLOCK
    left_group = lane < GROUP
    row_block = lax.broadcasted_iota(jnp.int32, (GROUP // BLOCK, BLOCK, LANES), 0) * BLOCK
    stores = []
    for n, span in enumerate(spans):
        for copy in loads[n]:
            copy.wait()
        if n == 0:
            for copy in (index_load, *table_loads):
                copy.wait()
        row_fwd, col_fwd, row_inv, col_inv = tables
        count = (span.stop - span.start) // LANES
        moment = DECAY * moment_buf[:, span] + grad_buf[:, span].astype(F32)
        mixed = mix_rows(row_fwd[...], moment)
        stacked = jnp.concatenate(
            [mixed[:, t * LANES : (t + 1) * LANES] for t in range(count)], axis=0
        )
        coefficients = mix_columns(stacked, col_fwd[...])
        start = half * steps * tiles * (LANES // GROUP) + span.start // GROUP
        kept = []
        for t in range(count):
            mask = None
            for k in range(KEEP):
                wanted = jnp.where(
                    left_group, picked[k, start + 2 * t], picked[k, start + 2 * t + 1]
                ) - lane_block
                hit = wanted[None] == row_block
                mask = hit if mask is None else mask | hit
            part = coefficients[t * GROUP : (t + 1) * GROUP].reshape(GROUP // BLOCK, BLOCK, LANES)
            kept.append(jnp.where(mask, part, 0.0).reshape(GROUP, LANES))
        unmixed = mix_columns(jnp.concatenate(kept, axis=0), col_inv[...])
        spread = jnp.concatenate(
            [unmixed[t * GROUP : (t + 1) * GROUP] for t in range(count)], axis=1
        )
        transmitted = mix_rows(row_inv[...], spread)
        new_buf[:, span] = moment - transmitted
        store = pltpu.make_async_copy(
            new_buf.at[:, span], new_momentum.at[0, :, columns(span)], out_sems.at[n]
        )
        store.start()
        stores.append(store)
        for j in range(span.start // wide, span.stop // wide):
            for i in range(GROUP // ROWS):
                goal = chunk_column(j, low)
                outer = jnp.where(half == 0, i, goal)
                inner = jnp.where(half == 0, goal, i)
                for t in range(tiles):
                    at = j * wide + t * LANES - span.start
                    part = transmitted[i * ROWS : (i + 1) * ROWS, at : at + LANES]
                    sent_buf[j, i, t] = part.astype(sent_buf.dtype)
                store = pltpu.make_async_copy(
                    sent_buf.at[j, i], sent.at[outer, inner], sent_sems.at[j, i]
                )
                store.start()
                stores.append(store)
    for store in stores:
        store.wait()


def compress(first, picked, momentum, gradient, tables, partial=None):
    _, height, breadth = momentum.shape
    steps = SIZES[1]
    wide = breadth // 2 // steps
    tiles = wide // LANES
    chunk = (tiles, ROWS, LANES)
    kind = BF16 if first else F32
    in_specs = [pl.BlockSpec(memory_space=pltpu.HBM)] * (3 + len(tables))
    out_shape = [
        jax.ShapeDtypeStruct((1, height, breadth), F32),
        jax.ShapeDtypeStruct((SIZES[0], steps) + chunk, kind),
    ]
    out_specs = [pl.BlockSpec(memory_space=pltpu.HBM)] * 2
    operands = [picked, momentum, gradient, *tables]
    aliases = {}
    if not first:
        aliases = {len(operands): 0}
        operands.append(partial)
        in_specs.append(pl.BlockSpec(memory_space=pltpu.HBM))

    def body(*refs):
        compress_kernel(first, tiles, steps, *refs)

    return pl.pallas_call(
        body,
        in_specs=in_specs,
        out_specs=out_specs,
        out_shape=out_shape,
        scratch_shapes=[
            pltpu.VMEM((height, steps * wide), F32),
            pltpu.VMEM((height, steps * wide), BF16),
            pltpu.VMEM((height, steps * wide), F32),
            *(pltpu.VMEM(table.shape, BF16) for table in tables),
            pltpu.SemaphoreType.DMA((steps, 2)),
            pltpu.SemaphoreType.DMA((steps,)),
            pltpu.SemaphoreType.DMA((5,)),
            pltpu.VMEM((steps, SIZES[0]) + chunk, kind),
            pltpu.SemaphoreType.DMA((steps, SIZES[0])),
            pltpu.SMEM(picked.shape, jnp.int32),
        ],
        input_output_aliases=aliases,
        compiler_params=pltpu.CompilerParams(vmem_limit_bytes=60 * 2**20),
        cost_estimate=pl.CostEstimate(
            flops=2 * 4 * 256 * height * breadth, bytes_accessed=6 * height * breadth, transcendentals=0
        ),
        name="compress_first" if first else "compress_second",
    )(*operands)


def row_shard(shard, low, k):
    return shard ^ k


def below_shard(shard, low, k):
    return 2 + (((shard + 1 - low) & 1) ^ k)


def above_shard(shard, low, k):
    return ((shard + low) & 1) ^ k


def own_part(weight, summed, scale):
    tiles, rows, lanes = summed.shape
    wide = tiles * lanes

    def body(weight, summed, out, held, sem):
        first, second, low, core = whereabouts()[:4]
        row = pl.multiple_of(first * rows, rows)
        at = pl.multiple_of((core * SIZES[1] + chunk_column(second, low)) * wide, wide)
        load = pltpu.make_async_copy(weight.at[pl.ds(row, rows), pl.ds(at, wide)], held, sem)
        load.start()
        load.wait()
        for t in range(tiles):
            own = held[:, t * lanes : (t + 1) * lanes].astype(F32)
            out[t] = own - scale * summed[t]

    return pl.pallas_call(
        body,
        in_specs=[pl.BlockSpec(memory_space=pltpu.HBM), pl.BlockSpec(memory_space=pltpu.VMEM)],
        out_specs=pl.BlockSpec(memory_space=pltpu.VMEM),
        out_shape=jax.ShapeDtypeStruct(summed.shape, F32),
        scratch_shapes=[pltpu.VMEM((rows, wide), BF16), pltpu.SemaphoreType.DMA],
        compiler_params=pltpu.CompilerParams(vmem_limit_bytes=16 * 2**20),
        name="own_part",
    )(weight, summed)


def project(tokens, pieces, own, steps, shards, breadth, partial=None):
    count, depth = tokens.shape
    _, side, tiles, rows, lanes = pieces[0].shape
    wide = tiles * lanes
    number = len(pieces)
    slots = sum(piece.shape[0] for piece in pieces)

    def body(tokens, *rest):
        place = whereabouts()
        arrays, (out, held, sems) = rest[:number], rest[-3:]
        first, second, low, core, mine = place
        turn_of, start = (first, second) if own else (second, first)
        start = chunk_column(start, low)
        half = core if own else 1 - core
        order = [lax.rem(turn_of - i + side, side) for i in range(side)]
        copies = []
        for n in range(number):
            at = half * side + lax.rem(start - steps[n] + side, side)
            for k in range(pieces[n].shape[0]):
                slot = len(copies)
                table = jnp.concatenate(
                    [
                        jnp.concatenate([arrays[n][k, order[i], t] for i in range(side)], axis=0)
                        for t in range(tiles)
                    ],
                    axis=1,
                )
                held[slot] = jnp.dot(
                    tokens[...], table, preferred_element_type=F32
                ).astype(BF16)
                column = pl.multiple_of((shards[n](mine, low, k) * 2 * side + at) * wide, wide)
                copy = pltpu.make_async_copy(
                    held.at[slot], out.at[:, pl.ds(column, wide)], sems.at[slot]
                )
                copy.start()
                copies.append(copy)
        for copy in copies:
            copy.wait()

    operands = [tokens, *pieces]
    in_specs = [pl.BlockSpec(memory_space=pltpu.VMEM)] * (1 + number)
    aliases = {}
    if partial is not None:
        aliases = {len(operands): 0}
        operands.append(partial)
        in_specs.append(pl.BlockSpec(memory_space=pltpu.HBM))
    return pl.pallas_call(
        body,
        in_specs=in_specs,
        out_specs=pl.BlockSpec(memory_space=pltpu.HBM),
        out_shape=jax.ShapeDtypeStruct((count, breadth), BF16),
        scratch_shapes=[
            pltpu.VMEM((slots, count, wide), BF16),
            pltpu.SemaphoreType.DMA((slots,)),
        ],
        input_output_aliases=aliases,
        compiler_params=pltpu.CompilerParams(vmem_limit_bytes=16 * 2**20),
        cost_estimate=pl.CostEstimate(
            flops=2 * count * depth * wide * slots,
            bytes_accessed=4 * count * wide * slots,
            transcendentals=0,
        ),
        name="project",
    )(*operands)


def after(preact, *values):
    def body(*refs):
        pass

    spaces = [pltpu.VMEM] * len(values) + [pltpu.HBM]
    operands = (*values, preact)
    return pl.pallas_call(
        body,
        in_specs=[pl.BlockSpec(memory_space=space) for space in spaces],
        out_specs=[pl.BlockSpec(memory_space=space) for space in spaces],
        out_shape=[jax.ShapeDtypeStruct(v.shape, v.dtype) for v in operands],
        input_output_aliases={n: n for n in range(len(operands))},
        compiler_params=pltpu.CompilerParams(vmem_limit_bytes=16 * 2**20),
        name="after",
    )(*operands)


def move(value, goal, *axes):
    extent = [lax.axis_size(axis) for axis in axes]
    places = list(np.ndindex(*extent))
    number = {spot: n for n, spot in enumerate(places)}
    pairs = []
    for spot in places:
        there = tuple(c % e for c, e in zip(goal(*spot), extent))
        pairs.append((number[spot], number[there]))
    return lax.ppermute(value, axes, pairs)


def swap(value):
    return move(value, lambda core: (core + 1,), "core")


def flip(value, mask):
    return move(value, lambda shard: (shard ^ mask,), "fsdp")


def turn(value, by, late):
    def goal(x, y, core):
        return (x + by, y, core) if (core == 0) != late else (x, y + by, core)

    return move(value, goal, "x", "y", "core")


def across(value):
    def goal(x, y, low, core):
        return (x, y + 2, low + 1, core) if core == 0 else (x + 2, y, low + 1, core)

    return move(value, goal, "x", "y", "zl", "core")


def climb(value, by):
    def goal(low, shard):
        z = 2 * shard + low + by
        return z % 2, z // 2

    return move(value, goal, "zl", "fsdp")


def on_device(momentum, gradient, weight, tokens, block_index):
    fsdp = lax.axis_size("fsdp")
    side = SIZES[0]
    plane = side * side
    full = fsdp * weight.shape[1]
    picked = block_index[0, 0].T
    cosines = cosine_table()
    tables = [
        jnp.asarray(left_operand(cosines)),
        jnp.asarray(right_operand(cosines.T)),
        jnp.asarray(left_operand(cosines.T)),
        jnp.asarray(right_operand(cosines)),
    ]
    partial, away = compress(True, picked, momentum, gradient, tables)
    arrived = swap(away)
    new_momentum, kept = compress(
        False, picked, momentum, gradient, tables, partial
    )
    pair = (kept + arrived.astype(F32)).astype(BF16)
    pair = pair.reshape((plane,) + pair.shape[2:])
    parts = lax.all_to_all(pair, ("x", "y"), 0, 0, tiled=True)
    summed = jnp.sum(parts.astype(F32), axis=0)
    scale = STEP / float(np.prod(SIZES))
    beyond = across(summed)
    chunk = (own_part(weight, summed, scale) - scale * beyond).astype(BF16)
    row = jnp.stack([chunk] + [flip(chunk, k) for k in range(1, fsdp)])
    stack = jnp.stack([row] + [turn(row, d, False) for d in range(1, side)], axis=1)
    left, right = turn(stack, 1, True), turn(stack, 3, True)
    near_half, far_half = stack[: fsdp // 2], stack[fsdp // 2 :]
    low_shards = lax.axis_index("fsdp") < fsdp // 2
    below = climb(jnp.where(low_shards, far_half, near_half), 1)
    above = climb(jnp.where(low_shards, near_half, far_half), -1)
    preact = project(tokens, [stack], True, (0,), (row_shard,), full)
    *arrays, preact = after(preact, stack, left, right, below, above)
    others = [swap(value) for value in arrays]
    steps = (0, 1, 3, 2, 2)
    shards = (row_shard, row_shard, row_shard, below_shard, above_shard)
    preact = project(tokens, arrays[1:], True, steps[1:], shards[1:], full, preact)
    preact = project(tokens, others, False, steps, shards, full, preact)
    return new_momentum, preact


def solution(mesh):
    split_mesh = Mesh(mesh.devices.reshape(SIZES + mesh.devices.shape[1:]), AXES)
    dp = AXES[:4]
    return jax.shard_map(
        on_device,
        mesh=split_mesh,
        in_specs=(
            P(dp, None, "fsdp"),
            P(dp, None, "fsdp"),
            P(None, "fsdp"),
            P(dp + ("fsdp",), None),
            P(dp, None, "fsdp", None),
        ),
        out_specs=(P(dp, None, "fsdp"), P(dp + ("fsdp",), None)),
        check_vma=False,
    )
```
